32 devices in a mesh: rep: 2 (over x), head: 8 (over z, y), req: 2 (over core).
Axes of the slice: x: 2, y: 2, z: 4, core: 2. Of those that a mesh axis runs over, the one named last changes fastest.
Arguments:
- hidden: bfloat16 [8, 512, 8192], P(('rep', 'req'), None, 'head'), parts along dimension 0, may hold values from -6 to 6
- lengths: int32 [8], P(('rep', 'req')), parts along dimension 0, may hold values from 128 to 512, as said below
- hit_slots: int32 [8], P('rep'), parts along dimension 0, may hold values from -1 to 15, as said below
- placement: int32 [8], P('rep'), parts along dimension 0, may hold values from 0 to 3, as said below
- state_pool: bfloat16 [32, 128, 64, 128], P(('rep', 'req'), 'head'), parts along dimension 0, may hold values from -3 to 3
- in_weight: bfloat16 [8192, 16512], P('req', 'head'), may hold values from -0.0625 to 0.0625
- group_weight: bfloat16 [8192, 1024], P('req', 'head'), may hold values from -0.0625 to 0.0625
- out_weight: bfloat16 [8192, 8192], P('head'), may hold values from -0.0625 to 0.0625
- decay_rate: float32 [128], P('head'), may hold values from 0.02 to 2
- step_bias: float32 [128], P('head'), may hold values from -4.6 to -3.2
- skip_gain: float32 [128], P('head'), may hold values from 0.5 to 1.5
Outputs:
- mixed: bfloat16 [8, 512, 8192], P(('rep', 'req'), None, 'head'), parts along dimension 0
- decode_states: bfloat16 [8, 128, 64, 128], P(('rep', 'req'), 'head'), parts along dimension 0
The draws below stay inside these ranges and needn't reach their ends.
There are 2 independent parts, one for each index of `rep`. The reference program is written for one: setup_inputs(seed, part) draws one part's arguments, and reference() takes and returns one part's arrays. A program takes and returns all parts, laid end to end along the dimension named above; an argument that names none is the same for every part. Nothing has to cross between parts.
Inputs may be any that keep to these rules, and one draw needn't show every extreme that they name: `lengths`: every live length lies in 128 .. 512 and one request of each part has 512. `hit_slots`: -1 marks a miss; slot s lives on req index s // 8; requests may share a slot. `placement`: a permutation of the requests; decode slot s lives on req index s // 2.
All inputs are finite; a program needn't handle non-finite values.
Results may differ from the reference program's by a relative error of at most 0.0076.
Values may be sent and summed in bfloat16 or wider, within the bound.
A program may use at most 256 MiB of HBM per device.

```python
import math
import jax
import jax.numpy as jnp
from jax import lax

D = 8192
H = 128
P_SIZE = 64
N = 128
G = 4
Q = 256
LEN = 512
COLS = 129
REQS = 4
SLOTS = 16


def draw_lengths(key, part):
    key = jax.random.fold_in(key, 3)
    first_key, second_key = jax.random.split(key)
    drawn = jax.random.randint(first_key, (REQS,), LEN // 4, LEN + 1)
    longest = jax.random.randint(second_key, (), 0, REQS)
    return jnp.where(jnp.arange(REQS) == longest, LEN, drawn).astype(jnp.int32)


def draw_hit_slots(key, part):
    key = jax.random.fold_in(key, 5)
    keys = jax.random.split(key, 4)
    drawn = jax.random.randint(keys[0], (REQS,), -1, SLOTS)
    chosen = jax.random.randint(keys[1], (), 0, REQS)
    partner = (chosen + jax.random.randint(keys[2], (), 1, REQS)) % REQS
    shared_slot = jax.random.randint(keys[3], (), 0, SLOTS)
    index = jnp.arange(REQS)
    missed = jnp.where(index == chosen, -1, drawn)
    sharing = jnp.where((index == chosen) | (index == partner), shared_slot, drawn)
    return jnp.where(part % 2 == 0, missed, sharing).astype(jnp.int32)


def draw_placement(key, part):
    key = jax.random.fold_in(key, 7)
    order = jax.random.permutation(key, REQS).astype(jnp.int32)
    return ((order + part) % REQS).astype(jnp.int32)


def levels(key, dims, shards, smallest, top_value):
    loudness, own = 1.0, jax.random.fold_in(key, 6)
    for position, parts in shards:
        steps = jnp.exp(jax.random.uniform(jax.random.fold_in(own, position), (parts,), jnp.float32, smallest / len(shards), top_value / len(shards)))
        loudness = loudness * jnp.repeat(steps, dims[position] // parts).reshape([-1 if axis == position else 1 for axis in range(len(dims))])
    return loudness


def scatter_about(key, dims, deviation, most, cuts=(), kind=jnp.bfloat16):
    gain = levels(key, dims, cuts, -0.22, 0.18) if cuts else 1.0
    values = jax.random.normal(key, dims, jnp.float32) * deviation * gain
    return jnp.minimum(jnp.maximum(values, -most), most).astype(kind)


def setup_inputs(seed: int = 0, part: int = 0) -> dict:
    key_list = jax.random.split(jax.random.key(seed), 12)
    part_keys = jax.random.split(jax.random.fold_in(key_list[11], part), 12)
    hidden = scatter_about(part_keys[0], (REQS, LEN, D), 1.0, 6.0, ((0, 2), (2, 8)))
    lengths = draw_lengths(jax.random.fold_in(jax.random.fold_in(key_list[11], part), 71), part)
    hit_slots = draw_hit_slots(jax.random.fold_in(jax.random.fold_in(key_list[11], part), 71), part)
    placement = draw_placement(jax.random.fold_in(jax.random.fold_in(key_list[11], part), 71), part)
    state_pool = scatter_about(part_keys[4], (SLOTS, H, P_SIZE, N), 0.5, 3.0, ((0, 2), (1, 8)))
    in_weight = scatter_about(key_list[5], (D, H * COLS), D ** -0.5, 0.0625, ((0, 2), (1, 8)))
    group_weight = scatter_about(key_list[6], (D, 2 * G * N), D ** -0.5, 0.0625, ((0, 2), (1, 8)))
    out_weight = scatter_about(key_list[7], (H * P_SIZE, D), (H * P_SIZE) ** -0.5, 0.0625, ((0, 8),))
    decay_rate = jnp.clip(jnp.exp(math.log(2.0) - 4.6051702 * jax.random.uniform(key_list[8], (H,), jnp.float32) ** levels(key_list[8], (H,), ((0, 8),), -0.2, 0.2)), 0.02, 2.0)
    step_bias = jnp.clip(-4.6 + 1.3999999 * jax.random.uniform(key_list[9], (H,), jnp.float32) ** levels(key_list[9], (H,), ((0, 8),), -0.2, 0.2), -4.6, -3.2)
    skip_gain = jnp.clip(0.5 + 1.0 * jax.random.uniform(key_list[10], (H,), jnp.float32) ** levels(key_list[10], (H,), ((0, 8),), -0.2, 0.2), 0.5, 1.5)
    return dict(hidden=hidden, lengths=lengths, hit_slots=hit_slots, placement=placement, state_pool=state_pool, in_weight=in_weight, group_weight=group_weight, out_weight=out_weight, decay_rate=decay_rate, step_bias=step_bias, skip_gain=skip_gain)


precise = lax.Precision.HIGHEST


def span_scan(inputs, step_sizes, b_heads, c_heads, decay_rates, initial):
    requests, length, head_count, head_width = inputs.shape
    state_size = b_heads.shape[-1]
    spans = length // Q
    x_span = inputs.reshape(requests, spans, Q, head_count, head_width)
    dt_span = step_sizes.reshape(requests, spans, Q, head_count)
    b_span = b_heads.reshape(requests, spans, Q, head_count, state_size)
    c_span = c_heads.reshape(requests, spans, Q, head_count, state_size)
    log_decay = jnp.cumsum(-dt_span * decay_rates, axis=2)
    within = jnp.arange(Q)[:, None] >= jnp.arange(Q)[None, :]
    spread = log_decay[:, :, :, None, :] - log_decay[:, :, None, :, :]
    decays = jnp.exp(jnp.where(within[None, None, :, :, None], spread, -jnp.inf))
    scores = jnp.einsum("bctkn,bcskn->bctsk", c_span, b_span, precision=precise)
    mixing = scores * decays * dt_span[:, :, None, :, :]
    intra_out = jnp.einsum("bctsk,bcskp->bctkp", mixing, x_span, precision=precise)
    to_end = jnp.exp(log_decay[:, :, -1:, :] - log_decay) * dt_span
    span_states = jnp.einsum("bcskp,bcskn->bckpn", x_span * to_end[..., None], b_span, precision=precise)
    through = jnp.exp(log_decay[:, :, -1, :])
    running = initial
    entering = []
    for span_index in range(spans):
        entering.append(running)
        running = through[:, span_index, :, None, None] * running + span_states[:, span_index]
    entering = jnp.stack(entering, axis=1)
    carried = jnp.exp(log_decay)[..., None] * jnp.einsum("bctkn,bckpn->bctkp", c_span, entering, precision=precise)
    return (intra_out + carried).reshape(requests, length, head_count, head_width), running


def reference(hidden, lengths, hit_slots, placement, state_pool, in_weight, group_weight, out_weight, decay_rate, step_bias, skip_gain):
    token_rows = REQS * LEN
    group_heads = H // G
    flat_tokens = hidden.reshape(token_rows, D)
    projected = jnp.dot(flat_tokens, in_weight, preferred_element_type=jnp.float32)
    projected = projected.reshape(REQS, LEN, H, COLS)
    inputs = projected[..., :P_SIZE].astype(jnp.bfloat16)
    gate_in = projected[..., P_SIZE:2 * P_SIZE].astype(jnp.bfloat16)
    step_raw = projected[..., 2 * P_SIZE]
    group_in = jnp.dot(flat_tokens, group_weight, preferred_element_type=jnp.float32).astype(jnp.bfloat16)
    group_in = group_in.reshape(REQS, LEN, G, 2 * N)
    b_groups = group_in[..., :N].astype(jnp.float32)
    c_groups = group_in[..., N:].astype(jnp.float32)
    live_mask = jnp.arange(LEN)[None, :] < lengths[:, None]
    step_sizes = jnp.where(live_mask[..., None], jax.nn.softplus(step_raw + step_bias), 0.0)
    fetched = state_pool[jnp.clip(hit_slots, 0, SLOTS - 1)].astype(jnp.float32)
    initial = jnp.where((hit_slots >= 0)[:, None, None, None], fetched, 0.0)
    inputs_f = inputs.astype(jnp.float32)

    def per_group(pieces):
        x_group, dt_group, b_group, c_group, rate_group, init_group = pieces
        b_heads = jnp.broadcast_to(b_group[:, :, None, :], (REQS, LEN, group_heads, N))
        c_heads = jnp.broadcast_to(c_group[:, :, None, :], (REQS, LEN, group_heads, N))
        return span_scan(x_group, dt_group, b_heads, c_heads, rate_group, init_group)

    stacked = (
        jnp.moveaxis(inputs_f.reshape(REQS, LEN, G, group_heads, P_SIZE), 2, 0),
        jnp.moveaxis(step_sizes.reshape(REQS, LEN, G, group_heads), 2, 0),
        jnp.moveaxis(b_groups, 2, 0),
        jnp.moveaxis(c_groups, 2, 0),
        decay_rate.reshape(G, group_heads),
        jnp.moveaxis(initial.reshape(REQS, G, group_heads, P_SIZE, N), 1, 0),
    )
    scanned, finals = lax.map(per_group, stacked)
    scanned = jnp.moveaxis(scanned, 0, 2).reshape(REQS, LEN, H, P_SIZE)
    finals = jnp.moveaxis(finals, 0, 1).reshape(REQS, H, P_SIZE, N)
    outputs = scanned + skip_gain[:, None] * inputs_f
    gated = jnp.where(live_mask[..., None, None], outputs * jax.nn.silu(gate_in.astype(jnp.float32)), 0.0)
    gated = gated.astype(jnp.bfloat16).reshape(token_rows, H * P_SIZE)
    mixed = jnp.dot(gated, out_weight, preferred_element_type=jnp.float32).astype(jnp.bfloat16).reshape(REQS, LEN, D)
    decode_states = jnp.zeros((REQS, H, P_SIZE, N), jnp.bfloat16).at[placement].set(finals.astype(jnp.bfloat16))
    return mixed, decode_states
```

```python
import functools
import jax
import jax.numpy as jnp
from jax import lax
from jax.experimental import pallas as pl
from jax.experimental.pallas import tpu as pltpu
from jax.sharding import PartitionSpec as P

P_SIZE = 64
N = 128
G = 4
Q = 256
PAIR = 2 * P_SIZE


def from_partner(value, axis, bit):
    mask = 2**bit
    pairs = [(source, source ^ mask) for source in range(lax.axis_size(axis))]
    return lax.ppermute(value, axis, pairs)


def scan_kernel(
    len_ref, x_ref, gate_ref, b_ref, c_ref, decay_ref, step_ref, row_ref, skip_ref, init_ref,
    out_ref, final_ref, scores_ref,
):
    spans = x_ref.shape[0] // Q
    t_index = lax.broadcasted_iota(jnp.int32, (Q, Q), 0)
    s_index = lax.broadcasted_iota(jnp.int32, (Q, Q), 1)

    @pl.when(pl.program_id(0) == 0)
    def _():
        for k in range(spans):
            rows = pl.ds(k * Q, Q)
            scores = lax.dot_general(
                c_ref[rows, :], b_ref[rows, :], (((1,), (1,)), ((), ())),
                preferred_element_type=jnp.float32,
            )
            scores_ref[k] = jnp.where(t_index >= s_index, scores, 0.0)

    first_lane = lax.broadcasted_iota(jnp.int32, (Q, PAIR), 1) < P_SIZE
    first_row = lax.broadcasted_iota(jnp.int32, (PAIR, N), 0) < P_SIZE
    position = lax.broadcasted_iota(jnp.int32, (Q, PAIR), 0)
    state = init_ref[...].astype(jnp.float32)
    for k in range(spans):
        rows = pl.ds(k * Q, Q)
        x = x_ref[rows, :].astype(jnp.float32)
        decay = decay_ref[rows, :]
        steps = step_ref[rows, :]
        stepped = x * steps
        stepped_cast = stepped.astype(jnp.bfloat16)
        scores = scores_ref[k]
        mixes = []
        for j in range(2):
            spread = decay[:, j * P_SIZE : j * P_SIZE + 1] - row_ref[0, j : j + 1, rows]
            weights = scores * jnp.exp(jnp.minimum(spread, 0.0))
            mixes.append(
                jnp.dot(
                    weights.astype(jnp.bfloat16), stepped_cast,
                    preferred_element_type=jnp.float32,
                )
            )
        intra = jnp.where(first_lane, mixes[0], mixes[1])
        carried = jnp.exp(decay) * lax.dot_general(
            c_ref[rows, :], state.astype(jnp.bfloat16), (((1,), (1,)), ((), ())),
            preferred_element_type=jnp.float32,
        )
        last = decay[Q - 1 : Q, :]
        leaving = (stepped * jnp.exp(last - decay)).astype(jnp.bfloat16)
        update = lax.dot_general(
            leaving, b_ref[rows, :], (((0,), (0,)), ((), ())),
            preferred_element_type=jnp.float32,
        )
        through = jnp.exp(
            jnp.where(first_row, last[:, :1], last[:, P_SIZE : P_SIZE + 1])
        )
        state = through * state + update
        gate = gate_ref[rows, :].astype(jnp.float32)
        value = (intra + carried + skip_ref[...] * x) * (gate * jax.nn.sigmoid(gate))
        live = position + k * Q < len_ref[0]
        out_ref[rows, :] = jnp.where(live, value, 0.0).astype(jnp.bfloat16)
    final_ref[...] = state.astype(jnp.bfloat16)


def scan(length, projected, decay, steps, skip, initial):
    tokens, head_count = steps.shape
    width = head_count * P_SIZE
    pairs = width // PAIR
    by_lane = lambda value: jnp.repeat(value, P_SIZE, axis=1)
    rows = decay.T.reshape(pairs, 2, tokens)
    column = lambda base: pl.BlockSpec((tokens, PAIR), lambda p: (0, base + p))
    fixed = lambda place: pl.BlockSpec((tokens, N), lambda p: (0, place))
    return pl.pallas_call(
        scan_kernel,
        grid=(pairs,),
        out_shape=(
            jax.ShapeDtypeStruct((tokens, width), jnp.bfloat16),
            jax.ShapeDtypeStruct((width, N), jnp.bfloat16),
        ),
        in_specs=[
            pl.BlockSpec(memory_space=pltpu.SMEM),
            column(0),
            column(pairs),
            fixed(2 * pairs),
            fixed(2 * pairs + 1),
            column(0),
            column(0),
            pl.BlockSpec((1, 2, tokens), lambda p: (p, 0, 0)),
            pl.BlockSpec((1, PAIR), lambda p: (0, p)),
            pl.BlockSpec((PAIR, N), lambda p: (p, 0)),
        ],
        out_specs=(column(0), pl.BlockSpec((PAIR, N), lambda p: (p, 0))),
        scratch_shapes=[pltpu.VMEM((tokens // Q, Q, Q), jnp.float32)],
        compiler_params=pltpu.CompilerParams(vmem_limit_bytes=32 * 1024 * 1024),
        cost_estimate=pl.CostEstimate(
            flops=pairs * tokens * 2 * PAIR * (2 * Q + 2 * N),
            bytes_accessed=tokens * width * 16,
            transcendentals=head_count * tokens * Q,
        ),
    )(length, projected, projected, projected, projected, by_lane(decay), by_lane(steps), rows,
      by_lane(skip[None, :]), initial)


def fetch_states(hit_slots, state_pool, local_requests):
    slot_count = state_pool.shape[0]
    local_slot = hit_slots - lax.axis_index("req") * slot_count
    selector = (local_slot[:, None] == jnp.arange(slot_count)[None, :]).astype(jnp.bfloat16)
    outgoing = jnp.dot(
        selector, state_pool.reshape(slot_count, -1), preferred_element_type=jnp.float32
    )
    outgoing = outgoing.astype(jnp.bfloat16).reshape((hit_slots.shape[0],) + state_pool.shape[1:])
    incoming = lax.all_to_all(outgoing, "req", split_axis=0, concat_axis=0, tiled=True)
    incoming = incoming.reshape((lax.axis_size("req"), local_requests) + state_pool.shape[1:])
    return jnp.sum(incoming.astype(jnp.float32), axis=0).astype(jnp.bfloat16)


def arrange_weights(in_weight, group_weight, head_count):
    group_devices = lax.axis_size("head") // G
    place = lax.axis_index("head") % group_devices
    for bit in range(group_devices.bit_length() - 1):
        partner = from_partner(group_weight, "head", bit)
        upper = place // (1 << bit) % 2 == 1
        group_weight = jnp.where(
            upper,
            jnp.concatenate([partner, group_weight], axis=1),
            jnp.concatenate([group_weight, partner], axis=1),
        )
    by_head = in_weight.reshape(in_weight.shape[0], head_count, -1)
    part = lambda low, high: by_head[:, :, low:high].reshape(in_weight.shape[0], -1)
    main = jnp.concatenate(
        [part(0, P_SIZE), part(P_SIZE, 2 * P_SIZE), group_weight], axis=1
    )
    step = part(2 * P_SIZE, 2 * P_SIZE + 1)
    whole = []
    upper = lax.axis_index("req") == 1
    for own in (main, step):
        other = from_partner(own, "req", 0)
        whole.append(
            jnp.where(
                upper,
                jnp.concatenate([other, own], axis=0),
                jnp.concatenate([own, other], axis=0),
            )
        )
    return whole


def body(
    hidden,
    lengths,
    hit_slots,
    placement,
    state_pool,
    in_weight,
    group_weight,
    out_weight,
    decay_rate,
    step_bias,
    skip_gain,
):
    local_requests, length, feature_piece = hidden.shape
    head_count = decay_rate.shape[0]
    rows = [
        lax.all_gather(hidden[r], "head", axis=1, tiled=True) for r in range(local_requests)
    ]
    main_weight, step_weight = arrange_weights(in_weight, group_weight, head_count)
    initial = fetch_states(hit_slots, state_pool, local_requests)
    out_blocks = out_weight.reshape(out_weight.shape[0], -1, feature_piece)
    mixed, finals = [], []
    for r in range(local_requests):
        projected = jnp.dot(rows[r], main_weight, preferred_element_type=jnp.float32)
        projected = projected.astype(jnp.bfloat16)
        step_raw = jnp.dot(rows[r], step_weight, preferred_element_type=jnp.float32)
        live = jnp.arange(length)[:, None] < lengths[r]
        steps = jnp.where(live, jax.nn.softplus(step_raw + step_bias), 0.0)
        decay = jnp.cumsum((-steps * decay_rate).reshape(-1, Q, head_count), axis=1)
        gated, final = scan(
            lengths[r][None],
            projected,
            decay.reshape(length, head_count),
            steps,
            skip_gain,
            initial[r].reshape(head_count * P_SIZE, N),
        )
        finals.append(final)
        partial = jnp.einsum(
            "tk,kjc->jtc", gated, out_blocks, preferred_element_type=jnp.float32
        ).astype(jnp.bfloat16)
        mixed.append(lax.psum_scatter(partial, "head", scatter_dimension=0, tiled=True))
    mixed = jnp.concatenate(mixed, axis=0)
    request_total = placement.shape[0]
    my_targets = lax.dynamic_slice_in_dim(
        placement, lax.axis_index("req") * local_requests, local_requests, 0
    )
    finals = jnp.stack(finals)
    leaving = jnp.zeros((request_total,) + finals.shape[1:], jnp.float32)
    for r in range(local_requests):
        chosen = jnp.arange(request_total)[:, None, None] == my_targets[r]
        leaving = leaving + jnp.where(chosen, finals[r].astype(jnp.float32), 0.0)
    leaving = leaving.astype(jnp.bfloat16)
    arrived = lax.all_to_all(leaving, "req", split_axis=0, concat_axis=0, tiled=True)
    arrived = arrived.reshape(lax.axis_size("req"), local_requests, head_count, P_SIZE, N)
    decode_states = jnp.sum(arrived.astype(jnp.float32), axis=0).astype(jnp.bfloat16)
    return (mixed, decode_states)


def solution(mesh):
    in_specs = (
        P(("rep", "req"), None, "head"),
        P(("rep", "req")),
        P("rep"),
        P("rep"),
        P(("rep", "req"), "head", None, None),
        P("req", "head"),
        P("req", "head"),
        P("head", None),
        P("head"),
        P("head"),
        P("head"),
    )
    out_specs = (P(("rep", "req"), None, "head"), P(("rep", "req"), "head", None, None))
    return jax.shard_map(body, mesh=mesh, in_specs=in_specs, out_specs=out_specs, check_vma=False)
```

```python
import functools
import jax
import jax.numpy as jnp
from jax import lax
from jax.experimental import pallas as pl
from jax.experimental.pallas import tpu as pltpu
from jax.sharding import PartitionSpec as P

P_SIZE = 64
N = 128
G = 4
Q = 256
PAIR = 2 * P_SIZE


def from_partner(value, axis, bit):
    mask = 2**bit
    pairs = [(source, source ^ mask) for source in range(lax.axis_size(axis))]
    return lax.ppermute(value, axis, pairs)


def scan_kernel(
    len_ref, x_ref, gate_ref, b_ref, c_ref, decay_ref, step_ref, row_ref, skip_ref, init_ref,
    out_ref, final_ref, scores_ref,
):
    spans = x_ref.shape[0] // Q
    t_index = lax.broadcasted_iota(jnp.int32, (Q, Q), 0)
    s_index = lax.broadcasted_iota(jnp.int32, (Q, Q), 1)

    @pl.when(pl.program_id(0) == 0)
    def _():
        for k in range(spans):
            rows = pl.ds(k * Q, Q)
            scores = lax.dot_general(
                c_ref[rows, :], b_ref[rows, :], (((1,), (1,)), ((), ())),
                preferred_element_type=jnp.float32,
            )
            scores_ref[k] = jnp.where(t_index >= s_index, scores, 0.0)

    first_lane = lax.broadcasted_iota(jnp.int32, (Q, PAIR), 1) < P_SIZE
    first_row = lax.broadcasted_iota(jnp.int32, (PAIR, N), 0) < P_SIZE
    position = lax.broadcasted_iota(jnp.int32, (Q, PAIR), 0)
    state = init_ref[...].astype(jnp.float32)
    for k in range(spans):
        rows = pl.ds(k * Q, Q)
        x = x_ref[rows, :].astype(jnp.float32)
        decay = decay_ref[rows, :]
        steps = step_ref[rows, :]
        stepped = x * steps
        stepped_cast = stepped.astype(jnp.bfloat16)
        scores = scores_ref[k]
        mixes = []
        for j in range(2):
            spread = decay[:, j * P_SIZE : j * P_SIZE + 1] - row_ref[0, j : j + 1, rows]
            weights = scores * jnp.exp(jnp.minimum(spread, 0.0))
            mixes.append(
                jnp.dot(
                    weights.astype(jnp.bfloat16), stepped_cast,
                    preferred_element_type=jnp.float32,
                )
            )
        intra = jnp.where(first_lane, mixes[0], mixes[1])
        carried = jnp.exp(decay) * lax.dot_general(
            c_ref[rows, :], state.astype(jnp.bfloat16), (((1,), (1,)), ((), ())),
            preferred_element_type=jnp.float32,
        )
        last = decay[Q - 1 : Q, :]
        leaving = (stepped * jnp.exp(last - decay)).astype(jnp.bfloat16)
        update = lax.dot_general(
            leaving, b_ref[rows, :], (((0,), (0,)), ((), ())),
            preferred_element_type=jnp.float32,
        )
        through = jnp.exp(
            jnp.where(first_row, last[:, :1], last[:, P_SIZE : P_SIZE + 1])
        )
        state = through * state + update
        gate = gate_ref[rows, :].astype(jnp.float32)
        value = (intra + carried + skip_ref[...] * x) * (gate * jax.nn.sigmoid(gate))
        live = position + k * Q < len_ref[0]
        out_ref[rows, :] = jnp.where(live, value, 0.0).astype(jnp.bfloat16)
    final_ref[...] = state.astype(jnp.bfloat16)


def scan(length, projected, decay, steps, skip, initial):
    tokens, head_count = steps.shape
    width = head_count * P_SIZE
    pairs = width // PAIR
    by_lane = lambda value: jnp.repeat(value, P_SIZE, axis=1)
    rows = decay.T.reshape(pairs, 2, tokens)
    column = lambda base: pl.BlockSpec((tokens, PAIR), lambda p: (0, base + p))
    fixed = lambda place: pl.BlockSpec((tokens, N), lambda p: (0, place))
    return pl.pallas_call(
        scan_kernel,
        grid=(pairs,),
        out_shape=(
            jax.ShapeDtypeStruct((tokens, width), jnp.bfloat16),
            jax.ShapeDtypeStruct((width, N), jnp.bfloat16),
        ),
        in_specs=[
            pl.BlockSpec(memory_space=pltpu.SMEM),
            column(0),
            column(pairs),
            fixed(2 * pairs),
            fixed(2 * pairs + 1),
            column(0),
            column(0),
            pl.BlockSpec((1, 2, tokens), lambda p: (p, 0, 0)),
            pl.BlockSpec((1, PAIR), lambda p: (0, p)),
            pl.BlockSpec((PAIR, N), lambda p: (p, 0)),
        ],
        out_specs=(column(0), pl.BlockSpec((PAIR, N), lambda p: (p, 0))),
        scratch_shapes=[pltpu.VMEM((tokens // Q, Q, Q), jnp.float32)],
        compiler_params=pltpu.CompilerParams(vmem_limit_bytes=32 * 1024 * 1024),
        cost_estimate=pl.CostEstimate(
            flops=pairs * tokens * 2 * PAIR * (2 * Q + 2 * N),
            bytes_accessed=tokens * width * 16,
            transcendentals=head_count * tokens * Q,
        ),
    )(length, projected, projected, projected, projected, by_lane(decay), by_lane(steps), rows,
      by_lane(skip[None, :]), initial)


def ring_place(index, n):
    if n != 8:
        return index
    return jnp.where(index % 2 == 0, index // 2, n - 1 - index // 2)


def ring_index(place, n):
    place = lax.rem(place + 2 * n, n)
    if n != 8:
        return place
    return jnp.where(place < n // 2, 2 * place, 2 * (n - 1 - place) + 1)


def sum_kernel(n, gated_ref, w_ref, out_ref, w_buf, partial, going, coming, w_sem, send_sem, recv_sem):
    piece = out_ref.shape[-1]
    chunk = gated_ref.shape[1] // 2
    place = ring_place(lax.axis_index("head"), n)
    ways = (1, -1)
    barrier = pltpu.get_barrier_semaphore()
    for way in ways:
        pl.semaphore_signal(
            barrier, inc=1, device_id={"head": ring_index(place + way, n)},
            device_id_type=pl.DeviceIdType.MESH,
        )
    pl.semaphore_wait(barrier, 2)

    def load(step, slot, d):
        block = ring_index(place - ways[d] * (step + 1), n)
        columns = pl.ds(pl.multiple_of(block * piece, piece), piece)
        return pltpu.make_async_copy(
            w_ref.at[:, columns], w_buf.at[slot, d], w_sem.at[slot, d]
        )

    def send(step, d, c):
        rows = pl.ds(c * chunk, chunk)
        return pltpu.make_async_remote_copy(
            src_ref=going.at[step, d, rows],
            dst_ref=coming.at[step, d, rows],
            send_sem=send_sem.at[step, d, c],
            recv_sem=recv_sem.at[step, d, c],
            device_id={"head": ring_index(place + ways[d], n)},
            device_id_type=pl.DeviceIdType.MESH,
        )

    for d in range(2):
        load(0, 0, d).start()

    def one_step(step, carry):
        slot = lax.rem(step, 2)

        @pl.when(step < n - 1)
        def _():
            for d in range(2):
                load(step + 1, 1 - slot, d).start()

        for d in range(2):
            load(step, slot, d).wait()
        for c in range(2):
            rows = pl.ds(c * chunk, chunk)
            for d in range(2):
                partial[d, rows, :] = jnp.dot(
                    gated_ref[d, rows, :], w_buf[slot, d], preferred_element_type=jnp.float32
                )
        for c in range(2):
            rows = pl.ds(c * chunk, chunk)
            for d in range(2):

                @pl.when(step == 0)
                def _():
                    going[0, d, rows, :] = partial[d, rows, :].astype(jnp.bfloat16)
                    send(0, d, c).start()

                @pl.when(jnp.logical_and(step > 0, step < n - 1))
                def _():
                    send(step - 1, d, c).wait_recv()
                    going[step, d, rows, :] = (
                        partial[d, rows, :] + coming[step - 1, d, rows, :].astype(jnp.float32)
                    ).astype(jnp.bfloat16)
                    send(step, d, c).start()

                @pl.when(step == n - 1)
                def _():
                    send(n - 2, d, c).wait_recv()
                    out_ref[d, rows, :] = (
                        partial[d, rows, :] + coming[n - 2, d, rows, :].astype(jnp.float32)
                    ).astype(jnp.bfloat16)

        return carry

    lax.fori_loop(0, n, one_step, 0)

    def drain(step, carry):
        for d in range(2):
            for c in range(2):
                send(step, d, c).wait_send()
        return carry

    lax.fori_loop(0, n - 1, drain, 0)


def output_sum(gated, out_weight, piece):
    n = lax.axis_size("head")
    requests, tokens, depth = gated.shape
    slots = (n - 1, requests, tokens, piece)
    return pl.pallas_call(
        functools.partial(sum_kernel, n),
        out_shape=jax.ShapeDtypeStruct((requests, tokens, piece), jnp.bfloat16),
        in_specs=[pl.BlockSpec(memory_space=pltpu.VMEM), pl.BlockSpec(memory_space=pl.ANY)],
        out_specs=pl.BlockSpec(memory_space=pltpu.VMEM),
        scratch_shapes=[
            pltpu.VMEM((2, 2, depth, piece), jnp.bfloat16),
            pltpu.VMEM((requests, tokens, piece), jnp.float32),
            pltpu.VMEM(slots, jnp.bfloat16),
            pltpu.VMEM(slots, jnp.bfloat16),
            pltpu.SemaphoreType.DMA((2, 2)),
            pltpu.SemaphoreType.DMA((n - 1, 2, 2)),
            pltpu.SemaphoreType.DMA((n - 1, 2, 2)),
        ],
        compiler_params=pltpu.CompilerParams(
            collective_id=0, has_side_effects=True, vmem_limit_bytes=54 * 1024 * 1024
        ),
        cost_estimate=pl.CostEstimate(
            flops=2 * requests * tokens * depth * piece * n,
            bytes_accessed=depth * piece * n * 2 + requests * tokens * piece * n * 16,
            transcendentals=0,
        ),
    )(gated, out_weight)


def fetch_states(hit_slots, state_pool, local_requests):
    slot_count = state_pool.shape[0]
    local_slot = hit_slots - lax.axis_index("req") * slot_count
    selector = (local_slot[:, None] == jnp.arange(slot_count)[None, :]).astype(jnp.bfloat16)
    outgoing = jnp.dot(
        selector, state_pool.reshape(slot_count, -1), preferred_element_type=jnp.float32
    )
    outgoing = outgoing.astype(jnp.bfloat16).reshape((hit_slots.shape[0],) + state_pool.shape[1:])
    incoming = lax.all_to_all(outgoing, "req", split_axis=0, concat_axis=0, tiled=True)
    incoming = incoming.reshape((lax.axis_size("req"), local_requests) + state_pool.shape[1:])
    return jnp.sum(incoming.astype(jnp.float32), axis=0).astype(jnp.bfloat16)


def arrange_weights(in_weight, group_weight, head_count):
    group_devices = lax.axis_size("head") // G
    place = lax.axis_index("head") % group_devices
    for bit in range(group_devices.bit_length() - 1):
        partner = from_partner(group_weight, "head", bit)
        upper = place // (1 << bit) % 2 == 1
        group_weight = jnp.where(
            upper,
            jnp.concatenate([partner, group_weight], axis=1),
            jnp.concatenate([group_weight, partner], axis=1),
        )
    by_head = in_weight.reshape(in_weight.shape[0], head_count, -1)
    part = lambda low, high: by_head[:, :, low:high].reshape(in_weight.shape[0], -1)
    main = jnp.concatenate(
        [part(0, P_SIZE), part(P_SIZE, 2 * P_SIZE), group_weight], axis=1
    )
    step = part(2 * P_SIZE, 2 * P_SIZE + 1)
    whole = []
    mine = lax.axis_index("req")
    for own in (main, step):
        depth, columns = own.shape
        other = from_partner(own, "req", 0)
        both = jnp.zeros((2, depth, columns), own.dtype)
        both = lax.dynamic_update_slice(both, own[None], (mine, 0, 0))
        both = lax.dynamic_update_slice(both, other[None], (1 - mine, 0, 0))
        whole.append(both.reshape(2 * depth, columns))
    return whole


def body(
    hidden,
    lengths,
    hit_slots,
    placement,
    state_pool,
    in_weight,
    group_weight,
    out_weight,
    decay_rate,
    step_bias,
    skip_gain,
):
    local_requests, length, feature_piece = hidden.shape
    head_count = decay_rate.shape[0]
    rows = [lax.all_gather(hidden[0], "head", axis=1, tiled=True)]
    main_weight, step_weight = arrange_weights(in_weight, group_weight, head_count)
    for r in range(1, local_requests):
        later, main_weight, step_weight = lax.optimization_barrier(
            (hidden[r], main_weight, step_weight)
        )
        rows.append(lax.all_gather(later, "head", axis=1, tiled=True))
    initial = fetch_states(hit_slots, state_pool, local_requests)
    gated_all, finals = [], []
    for r in range(local_requests):
        projected = jnp.dot(rows[r], main_weight, preferred_element_type=jnp.float32)
        projected = projected.astype(jnp.bfloat16)
        step_raw = jnp.dot(rows[r], step_weight, preferred_element_type=jnp.float32)
        live = jnp.arange(length)[:, None] < lengths[r]
        steps = jnp.where(live, jax.nn.softplus(step_raw + step_bias), 0.0)
        decay = jnp.cumsum((-steps * decay_rate).reshape(-1, Q, head_count), axis=1)
        gated, final = scan(
            lengths[r][None],
            projected,
            decay.reshape(length, head_count),
            steps,
            skip_gain,
            initial[r].reshape(head_count * P_SIZE, N),
        )
        finals.append(final)
        gated_all.append(gated)
    mixed = output_sum(jnp.stack(gated_all), out_weight, feature_piece)
    request_total = placement.shape[0]
    my_targets = lax.dynamic_slice_in_dim(
        placement, lax.axis_index("req") * local_requests, local_requests, 0
    )
    finals = jnp.stack(finals)
    leaving = jnp.zeros((request_total,) + finals.shape[1:], jnp.float32)
    for r in range(local_requests):
        chosen = jnp.arange(request_total)[:, None, None] == my_targets[r]
        leaving = leaving + jnp.where(chosen, finals[r].astype(jnp.float32), 0.0)
    leaving = leaving.astype(jnp.bfloat16)
    arrived = lax.all_to_all(leaving, "req", split_axis=0, concat_axis=0, tiled=True)
    arrived = arrived.reshape(lax.axis_size("req"), local_requests, head_count, P_SIZE, N)
    decode_states = jnp.sum(arrived.astype(jnp.float32), axis=0).astype(jnp.bfloat16)
    return (mixed, decode_states)


def solution(mesh):
    in_specs = (
        P(("rep", "req"), None, "head"),
        P(("rep", "req")),
        P("rep"),
        P("rep"),
        P(("rep", "req"), "head", None, None),
        P("req", "head"),
        P("req", "head"),
        P("head", None),
        P("head"),
        P("head"),
        P("head"),
    )
    out_specs = (P(("rep", "req"), None, "head"), P(("rep", "req"), "head", None, None))
    return jax.shard_map(body, mesh=mesh, in_specs=in_specs, out_specs=out_specs, check_vma=False)
```

```python
import functools
import jax
import jax.numpy as jnp
from jax import lax
from jax.experimental import pallas as pl
from jax.experimental.pallas import tpu as pltpu
from jax.sharding import PartitionSpec as P

P_SIZE = 64
N = 128
G = 4
Q = 256
PAIR = 2 * P_SIZE


def from_partner(value, axis, bit):
    mask = 2**bit
    pairs = [(source, source ^ mask) for source in range(lax.axis_size(axis))]
    return lax.ppermute(value, axis, pairs)


def scan_kernel(
    len_ref, x_ref, gate_ref, b_ref, c_ref, decay_ref, step_ref, row_ref, skip_ref, init_ref,
    out_ref, final_ref, scores_ref,
):
    spans = x_ref.shape[0] // Q
    t_index = lax.broadcasted_iota(jnp.int32, (Q, Q), 0)
    s_index = lax.broadcasted_iota(jnp.int32, (Q, Q), 1)

    @pl.when(pl.program_id(0) == 0)
    def _():
        for k in range(spans):
            rows = pl.ds(k * Q, Q)
            scores = lax.dot_general(
                c_ref[rows, :], b_ref[rows, :], (((1,), (1,)), ((), ())),
                preferred_element_type=jnp.float32,
            )
            scores_ref[k] = jnp.where(t_index >= s_index, scores, 0.0)

    first_lane = lax.broadcasted_iota(jnp.int32, (Q, PAIR), 1) < P_SIZE
    first_row = lax.broadcasted_iota(jnp.int32, (PAIR, N), 0) < P_SIZE
    position = lax.broadcasted_iota(jnp.int32, (Q, PAIR), 0)
    state = init_ref[...].astype(jnp.float32)
    for k in range(spans):
        rows = pl.ds(k * Q, Q)
        x = x_ref[rows, :].astype(jnp.float32)
        decay = decay_ref[rows, :]
        steps = step_ref[rows, :]
        stepped = x * steps
        stepped_cast = stepped.astype(jnp.bfloat16)
        scores = scores_ref[k]
        mixes = []
        for j in range(2):
            spread = decay[:, j * P_SIZE : j * P_SIZE + 1] - row_ref[0, j : j + 1, rows]
            weights = scores * jnp.exp(jnp.minimum(spread, 0.0))
            mixes.append(
                jnp.dot(
                    weights.astype(jnp.bfloat16), stepped_cast,
                    preferred_element_type=jnp.float32,
                )
            )
        intra = jnp.where(first_lane, mixes[0], mixes[1])
        carried = jnp.exp(decay) * lax.dot_general(
            c_ref[rows, :], state.astype(jnp.bfloat16), (((1,), (1,)), ((), ())),
            preferred_element_type=jnp.float32,
        )
        last = decay[Q - 1 : Q, :]
        leaving = (stepped * jnp.exp(last - decay)).astype(jnp.bfloat16)
        update = lax.dot_general(
            leaving, b_ref[rows, :], (((0,), (0,)), ((), ())),
            preferred_element_type=jnp.float32,
        )
        through = jnp.exp(
            jnp.where(first_row, last[:, :1], last[:, P_SIZE : P_SIZE + 1])
        )
        state = through * state + update
        gate = gate_ref[rows, :].astype(jnp.float32)
        value = (intra + carried + skip_ref[...] * x) * (gate * jax.nn.sigmoid(gate))
        live = position + k * Q < len_ref[0]
        out_ref[rows, :] = jnp.where(live, value, 0.0).astype(jnp.bfloat16)
    final_ref[...] = state.astype(jnp.bfloat16)


def scan(length, projected, decay, steps, skip, initial):
    tokens, head_count = steps.shape
    width = head_count * P_SIZE
    pairs = width // PAIR
    by_lane = lambda value: jnp.repeat(value, P_SIZE, axis=1)
    rows = decay.T.reshape(pairs, 2, tokens)
    column = lambda base: pl.BlockSpec((tokens, PAIR), lambda p: (0, base + p))
    fixed = lambda place: pl.BlockSpec((tokens, N), lambda p: (0, place))
    return pl.pallas_call(
        scan_kernel,
        grid=(pairs,),
        out_shape=(
            jax.ShapeDtypeStruct((tokens, width), jnp.bfloat16),
            jax.ShapeDtypeStruct((width, N), jnp.bfloat16),
        ),
        in_specs=[
            pl.BlockSpec(memory_space=pltpu.SMEM),
            column(0),
            column(pairs),
            fixed(2 * pairs),
            fixed(2 * pairs + 1),
            column(0),
            column(0),
            pl.BlockSpec((1, 2, tokens), lambda p: (p, 0, 0)),
            pl.BlockSpec((1, PAIR), lambda p: (0, p)),
            pl.BlockSpec((PAIR, N), lambda p: (p, 0)),
        ],
        out_specs=(column(0), pl.BlockSpec((PAIR, N), lambda p: (p, 0))),
        scratch_shapes=[pltpu.VMEM((tokens // Q, Q, Q), jnp.float32)],
        compiler_params=pltpu.CompilerParams(vmem_limit_bytes=32 * 1024 * 1024),
        cost_estimate=pl.CostEstimate(
            flops=pairs * tokens * 2 * PAIR * (2 * Q + 2 * N),
            bytes_accessed=tokens * width * 16,
            transcendentals=head_count * tokens * Q,
        ),
    )(length, projected, projected, projected, projected, by_lane(decay), by_lane(steps), rows,
      by_lane(skip[None, :]), initial)


def ring_place(index, n):
    if n != 8:
        return index
    return jnp.where(index % 2 == 0, index // 2, n - 1 - index // 2)


def ring_index(place, n):
    place = lax.rem(place + 2 * n, n)
    if n != 8:
        return place
    return jnp.where(place < n // 2, 2 * place, 2 * (n - 1 - place) + 1)


def sum_kernel(n, gated_ref, w_ref, out_ref, w_buf, partial, going, coming, w_sem, send_sem, recv_sem):
    piece = out_ref.shape[-1]
    chunk = gated_ref.shape[1] // 2
    place = ring_place(lax.axis_index("head"), n)
    ways = (1, -1)
    barrier = pltpu.get_barrier_semaphore()
    for way in ways:
        pl.semaphore_signal(
            barrier, inc=1, device_id={"head": ring_index(place + way, n)},
            device_id_type=pl.DeviceIdType.MESH,
        )
    pl.semaphore_wait(barrier, 2)

    def load(step, slot, d):
        block = ring_index(place - ways[d] * (step + 1), n)
        columns = pl.ds(pl.multiple_of(block * piece, piece), piece)
        return pltpu.make_async_copy(
            w_ref.at[:, columns], w_buf.at[slot, d], w_sem.at[slot, d]
        )

    def send(step, d, c):
        rows = pl.ds(c * chunk, chunk)
        return pltpu.make_async_remote_copy(
            src_ref=going.at[step, d, rows],
            dst_ref=coming.at[step, d, rows],
            send_sem=send_sem.at[step, d, c],
            recv_sem=recv_sem.at[step, d, c],
            device_id={"head": ring_index(place + ways[d], n)},
            device_id_type=pl.DeviceIdType.MESH,
        )

    for d in range(2):
        load(0, 0, d).start()

    def one_step(step, carry):
        slot = lax.rem(step, 2)

        @pl.when(step < n - 1)
        def _():
            for d in range(2):
                load(step + 1, 1 - slot, d).start()

        for d in range(2):
            load(step, slot, d).wait()
        for c in range(2):
            rows = pl.ds(c * chunk, chunk)
            for d in range(2):
                partial[d, rows, :] = jnp.dot(
                    gated_ref[d, rows, :], w_buf[slot, d], preferred_element_type=jnp.float32
                )
        for c in range(2):
            rows = pl.ds(c * chunk, chunk)
            for d in range(2):

                @pl.when(step == 0)
                def _():
                    going[0, d, rows, :] = partial[d, rows, :].astype(jnp.bfloat16)
                    send(0, d, c).start()

                @pl.when(jnp.logical_and(step > 0, step < n - 1))
                def _():
                    send(step - 1, d, c).wait_recv()
                    going[step, d, rows, :] = (
                        partial[d, rows, :] + coming[step - 1, d, rows, :].astype(jnp.float32)
                    ).astype(jnp.bfloat16)
                    send(step, d, c).start()

                @pl.when(step == n - 1)
                def _():
                    send(n - 2, d, c).wait_recv()
                    out_ref[d, rows, :] = (
                        partial[d, rows, :] + coming[n - 2, d, rows, :].astype(jnp.float32)
                    ).astype(jnp.bfloat16)

        return carry

    lax.fori_loop(0, n, one_step, 0)

    def drain(step, carry):
        for d in range(2):
            for c in range(2):
                send(step, d, c).wait_send()
        return carry

    lax.fori_loop(0, n - 1, drain, 0)


def output_sum(gated, out_weight, piece):
    n = lax.axis_size("head")
    requests, tokens, depth = gated.shape
    slots = (n - 1, requests, tokens, piece)
    return pl.pallas_call(
        functools.partial(sum_kernel, n),
        out_shape=jax.ShapeDtypeStruct((requests, tokens, piece), jnp.bfloat16),
        in_specs=[pl.BlockSpec(memory_space=pltpu.VMEM), pl.BlockSpec(memory_space=pl.ANY)],
        out_specs=pl.BlockSpec(memory_space=pltpu.VMEM),
        scratch_shapes=[
            pltpu.VMEM((2, 2, depth, piece), jnp.bfloat16),
            pltpu.VMEM((requests, tokens, piece), jnp.float32),
            pltpu.VMEM(slots, jnp.bfloat16),
            pltpu.VMEM(slots, jnp.bfloat16),
            pltpu.SemaphoreType.DMA((2, 2)),
            pltpu.SemaphoreType.DMA((n - 1, 2, 2)),
            pltpu.SemaphoreType.DMA((n - 1, 2, 2)),
        ],
        compiler_params=pltpu.CompilerParams(
            collective_id=0, has_side_effects=True, vmem_limit_bytes=54 * 1024 * 1024
        ),
        cost_estimate=pl.CostEstimate(
            flops=2 * requests * tokens * depth * piece * n,
            bytes_accessed=depth * piece * n * 2 + requests * tokens * piece * n * 16,
            transcendentals=0,
        ),
    )(gated, out_weight)


def fetch_states(hit_slots, state_pool, local_requests):
    slot_count = state_pool.shape[0]
    local_slot = hit_slots - lax.axis_index("req") * slot_count
    selector = (local_slot[:, None] == jnp.arange(slot_count)[None, :]).astype(jnp.bfloat16)
    outgoing = jnp.dot(
        selector, state_pool.reshape(slot_count, -1), preferred_element_type=jnp.float32
    )
    outgoing = outgoing.astype(jnp.bfloat16).reshape((hit_slots.shape[0],) + state_pool.shape[1:])
    incoming = lax.all_to_all(outgoing, "req", split_axis=0, concat_axis=0, tiled=True)
    incoming = incoming.reshape((lax.axis_size("req"), local_requests) + state_pool.shape[1:])
    return jnp.sum(incoming.astype(jnp.float32), axis=0).astype(jnp.bfloat16)


def join_group(group_weight):
    group_devices = lax.axis_size("head") // G
    place = lax.axis_index("head") % group_devices
    for bit in range(group_devices.bit_length() - 1):
        partner = from_partner(group_weight, "head", bit)
        upper = place // (1 << bit) % 2 == 1
        group_weight = jnp.where(
            upper,
            jnp.concatenate([partner, group_weight], axis=1),
            jnp.concatenate([group_weight, partner], axis=1),
        )
    return group_weight


def split_heads(in_weight, head_count):
    return in_weight.reshape(in_weight.shape[0], head_count, -1)


def take_parts(by_head):
    part = lambda low, high: by_head[:, :, low:high].reshape(by_head.shape[0], -1)
    return (
        part(0, P_SIZE),
        part(P_SIZE, 2 * P_SIZE),
        part(2 * P_SIZE, 2 * P_SIZE + 1),
    )


def tied(first, second):
    return lax.optimization_barrier((first, second))


def ring_gather(hidden, in_weight, group_weight, head_count):
    n = lax.axis_size("head")
    requests, tokens, piece = hidden.shape
    places = [int(p) for p in range(n)]
    index_of = [p if n != 8 else (2 * p if p < n // 2 else 2 * (n - 1 - p) + 1) for p in places]
    place = ring_place(lax.axis_index("head"), n)
    first = lax.axis_index("req") * (n // 2)
    held = [hidden[r] for r in range(requests)]
    group_weight = join_group(group_weight)
    stage = in_weight
    whole = [jnp.zeros((tokens, n * piece), hidden.dtype) for _ in range(requests)]
    for step in range(n):
        for r in range(requests):
            way = 1 if r % 2 == 0 else -1
            owner = ring_index(place - way * step, n)
            column = lax.rem(owner + first, n) * piece
            whole[r] = lax.dynamic_update_slice(whole[r], held[r], (0, column))
            if step < n - 1:
                pairs = [(index_of[p], index_of[(p + way) % n]) for p in places]
                held[r] = lax.ppermute(held[r], "head", pairs)
        if step < 4:
            held, stage = tied(held, stage)
            if step == 0:
                next_stage = split_heads(stage, head_count)
            elif step == 1:
                next_stage = take_parts(stage)
            elif step == 2:
                x_part, gate_part, step_part = stage
                main = jnp.concatenate([x_part, gate_part, group_weight], axis=1)
                next_stage = (main, step_part)
            else:
                next_stage = stage
            stage = next_stage
    main, step_part = stage
    halves = [(own, from_partner(own, "req", 0)) for own in (main, step_part)]
    return whole, halves


def by_halves(rows, halves):
    half = rows.shape[1] // 2
    return jnp.dot(
        rows[:, :half], halves[0], preferred_element_type=jnp.float32
    ) + jnp.dot(rows[:, half:], halves[1], preferred_element_type=jnp.float32)


def body(
    hidden,
    lengths,
    hit_slots,
    placement,
    state_pool,
    in_weight,
    group_weight,
    out_weight,
    decay_rate,
    step_bias,
    skip_gain,
):
    local_requests, length, feature_piece = hidden.shape
    head_count = decay_rate.shape[0]
    rows, (main_weight, step_weight) = ring_gather(
        hidden, in_weight, group_weight, head_count
    )
    initial = fetch_states(hit_slots, state_pool, local_requests)
    gated_all, finals = [], []
    for r in range(local_requests):
        projected = by_halves(rows[r], main_weight)
        projected = projected.astype(jnp.bfloat16)
        step_raw = by_halves(rows[r], step_weight)
        live = jnp.arange(length)[:, None] < lengths[r]
        steps = jnp.where(live, jax.nn.softplus(step_raw + step_bias), 0.0)
        decay = jnp.cumsum((-steps * decay_rate).reshape(-1, Q, head_count), axis=1)
        gated, final = scan(
            lengths[r][None],
            projected,
            decay.reshape(length, head_count),
            steps,
            skip_gain,
            initial[r].reshape(head_count * P_SIZE, N),
        )
        finals.append(final)
        gated_all.append(gated)
    mixed = output_sum(jnp.stack(gated_all), out_weight, feature_piece)
    request_total = placement.shape[0]
    my_targets = lax.dynamic_slice_in_dim(
        placement, lax.axis_index("req") * local_requests, local_requests, 0
    )
    finals = jnp.stack(finals)
    leaving = jnp.zeros((request_total,) + finals.shape[1:], jnp.float32)
    for r in range(local_requests):
        chosen = jnp.arange(request_total)[:, None, None] == my_targets[r]
        leaving = leaving + jnp.where(chosen, finals[r].astype(jnp.float32), 0.0)
    leaving = leaving.astype(jnp.bfloat16)
    arrived = lax.all_to_all(leaving, "req", split_axis=0, concat_axis=0, tiled=True)
    arrived = arrived.reshape(lax.axis_size("req"), local_requests, head_count, P_SIZE, N)
    decode_states = jnp.sum(arrived.astype(jnp.float32), axis=0).astype(jnp.bfloat16)
    return (mixed, decode_states)


def solution(mesh):
    in_specs = (
        P(("rep", "req"), None, "head"),
        P(("rep", "req")),
        P("rep"),
        P("rep"),
        P(("rep", "req"), "head", None, None),
        P("req", "head"),
        P("req", "head"),
        P("head", None),
        P("head"),
        P("head"),
        P("head"),
    )
    out_specs = (P(("rep", "req"), None, "head"), P(("rep", "req"), "head", None, None))
    return jax.shard_map(body, mesh=mesh, in_specs=in_specs, out_specs=out_specs, check_vma=False)
```
